1024 devices in a mesh: expert: 32 (over x_hi, y, core), dp: 32 (over x_lo, z).
Axes of the slice: x: 4 (x_hi: 2, x_lo: 2; x = x_hi * 2 + x_lo), y: 8, z: 16, core: 2. Of those that a mesh axis runs over, the one named last changes fastest.
Arguments:
- tokens: bfloat16 [6144, 4096], P('expert', 'dp'), may hold values from -6 to 6
- out_grad: bfloat16 [6144, 4096], P('expert', 'dp'), may hold values from -6 to 6
- routes: int32 [6144, 8], P('expert'), may hold values from 0 to 127, all different within a row; in each aligned block of 192 rows (0 to 191, 192 to 383, ...) at most 24 rows name the same one
- scores: float32 [6144, 8], P('expert'), may hold values from 0.05 to 1
- w_gate_up: bfloat16 [32, 4096, 2, 768], P('expert', 'dp'), may hold values from -0.09375 to 0.09375
- w_down: bfloat16 [32, 768, 4096], P('expert', None, 'dp'), may hold values from -0.21875 to 0.21875
Outputs:
- layer_out: bfloat16 [6144, 4096], P('expert', 'dp')
- grad_tokens: bfloat16 [6144, 4096], P('expert', 'dp')
- grad_gate_up: bfloat16 [32, 4096, 2, 768], P('expert', 'dp')
- grad_down: bfloat16 [32, 768, 4096], P('expert', None, 'dp')
The draws below stay inside these ranges and needn't reach their ends.
Inputs may be any that keep to these rules, and one draw needn't show every extreme that they name: `routes`: in each aligned block of 192 rows (the rows of one index of expert) no id is named by more than 24 rows, a bound that some block reaches.
All inputs are finite; a program needn't handle non-finite values.
Results may differ from the reference program's by a relative error of at most 0.0065.
Values may be sent and summed in bfloat16 or wider, within the bound.
A program may use at most 64 MiB of HBM per device.

```python
import math
import jax
import jax.numpy as jnp
import numpy as np
from jax import lax

D = 4096
ALL_EXPERTS = 128
TOP = 8
HID = 768
TOK_DEV = 192
CAP = 24
EXPERTS = 32
TOKENS = 6144
N_EXPERT = 32


def steps_of(stream_key, dims, shards, least, high):
    def one(axis_at, shards_of):
        heights = jax.random.uniform(jax.random.fold_in(jax.random.fold_in(stream_key, 6), axis_at), (shards_of,), jnp.float32, least / len(shards), high / len(shards))
        return jnp.repeat(jnp.exp(heights), dims[axis_at] // shards_of).reshape((-1,) + (1,) * (len(dims) - axis_at - 1))

    factor_of = one(*shards[0])
    for cut in shards[1:]:
        factor_of = factor_of * one(*cut)
    return factor_of


def shared_out(key, own, number, rows, number_of, top, reach, skew):
    ranking = jax.random.permutation(key, number_of)
    heavy_load, common = portions_of(number_of, rows * top, reach, skew, True), portions_of(number_of, rows * top, reach, skew, False)
    places = jnp.arange(number_of)

    def named(tallies, turn):
        used = int((tallies > 0).sum())
        fixed = max(1, used // 4)
        shifted = fixed + (places - fixed + turn * (used - fixed)) % max(1, number_of - fixed)
        return jnp.zeros((number_of,), jnp.int32).at[ranking[jnp.where(places < fixed, places, shifted)]].set(jnp.asarray(tallies, jnp.int32))

    tallies = jnp.where(number % 4 == 0, named(heavy_load, number // 4), named(common, number - number // 4 - 1))
    mixed = jax.random.permutation(jax.random.fold_in(own, 3), number_of)
    source_of, sink = mixed[0:number_of // 2 * 2:2], mixed[1:number_of // 2 * 2:2]
    slack = jnp.minimum(tallies[source_of] - 1, reach - tallies[sink]) // 2
    slack = jnp.where((source_of == ranking[0]) | (sink == ranking[0]) | (tallies[sink] == 0), 0, jnp.maximum(slack, 0))
    shifted = jax.random.randint(jax.random.fold_in(own, 4), (number_of // 2,), 0, 1 << 20) % (slack + 1)
    tallies = tallies.at[source_of].add(-shifted).at[sink].add(shifted)
    members = jnp.searchsorted(jnp.cumsum(tallies), jnp.arange(rows * top), side="right").astype(jnp.int32)
    listing = members.reshape(top, rows).T
    listing = listing[jax.random.permutation(jax.random.fold_in(own, 1), rows)]
    turn = jax.random.randint(jax.random.fold_in(own, 2), (rows, 1), 0, top)
    return jnp.take_along_axis(listing, (jnp.arange(top)[None, :] + turn) % top, axis=1)


def portions_of(number_of, total, bound, skew, full):
    portions = [(1 << 20) // math.isqrt(rank ** skew) + 1 for rank in range(1, number_of + 1)]
    largest = bound if full else min(bound, max(-(-total // number_of), total * portions[0] // sum(portions)))
    least = 1 if total - largest >= number_of - 1 else 0
    counts, spare = [largest] + [least] * (number_of - 1), total - largest - least * (number_of - 1)
    while spare > 0:
        movable = [i for i in range(1, number_of) if counts[i] < largest] or [i for i in range(1, number_of) if counts[i] < bound]
        pool, remaining = sum([portions[i] for i in movable]), spare
        for i in movable:
            more = min(bound - counts[i], max(1, remaining * portions[i] // pool), spare)
            counts[i] = counts[i] + more
            spare = spare - more
    return np.array(counts)


def gaussian(own_key, extent, deviation, limit, pieces=(), kind=jnp.bfloat16):
    values = deviation * jax.random.normal(own_key, extent, jnp.float32)
    if pieces:
        values = values * steps_of(own_key, extent, pieces, -0.22, 0.18)
    return jnp.clip(values, -limit, limit).astype(kind)


def setup_inputs(seed: int = 0) -> dict:
    key_of = jax.random.split(jax.random.key(seed), 7)
    tokens = gaussian(key_of[0], (TOKENS, D), 1.0, 6.0, ((0, 32), (1, 32)))
    out_grad = gaussian(key_of[1], (TOKENS, D), 1.0, 6.0, ((0, 32), (1, 32)))
    routes_keys = jax.random.split(jax.random.fold_in(key_of[2], 1), TOKENS // TOK_DEV)
    routes_turns = jax.random.permutation(jax.random.fold_in(key_of[2], 3), TOKENS // TOK_DEV)
    routes = jax.vmap(lambda own, number: shared_out(jax.random.fold_in(key_of[2], 2), own, number, TOK_DEV, ALL_EXPERTS, TOP, CAP, 2))(routes_keys, routes_turns).reshape((TOKENS, TOP))
    scores = jnp.clip(jnp.exp(math.log(1.0) - 2.9957323 * jax.random.uniform(key_of[3], (TOKENS, TOP), jnp.float32) ** steps_of(key_of[3], (TOKENS, TOP), ((0, 32),), -0.2, 0.2)), 0.05, 1.0)
    w_gate_up = gaussian(key_of[4], (EXPERTS, D, 2, HID), D ** -0.5, 0.09375, ((0, 32), (1, 32)))
    w_down = gaussian(key_of[5], (EXPERTS, HID, D), HID ** -0.5, 0.21875, ((0, 32), (2, 32)))
    return {"tokens": tokens, "out_grad": out_grad, "routes": routes, "scores": scores, "w_gate_up": w_gate_up, "w_down": w_down}


def reference(tokens, out_grad, routes, scores, w_gate_up, w_down):
    slots = N_EXPERT * CAP
    combine = scores / jnp.sum(scores, axis=1, keepdims=True)
    flat_ids = routes.reshape(-1)
    flat_weight = combine.reshape(-1)

    def one_expert(carry, expert):
        out_sum, grad_sum = carry
        hits = flat_ids == expert
        count = jnp.sum(hits.astype(jnp.int32))
        picks = jnp.nonzero(hits, size=slots, fill_value=0)[0].astype(jnp.int32)
        valid = jnp.arange(slots, dtype=jnp.int32) < count
        token_index = picks // TOP
        rows_in = tokens[token_index]
        weight = jnp.where(valid, flat_weight[picks], jnp.float32(0.0))
        pick_grad = (weight[:, None] * out_grad[token_index].astype(jnp.float32)).astype(jnp.bfloat16)
        first = lax.dynamic_index_in_dim(w_gate_up, expert, 0, keepdims=False)
        second = lax.dynamic_index_in_dim(w_down, expert, 0, keepdims=False)
        first_flat = first.reshape(D, 2 * HID)
        pre = jnp.dot(rows_in, first_flat, preferred_element_type=jnp.float32).reshape(slots, 2, HID)
        gate = pre[:, 0, :]
        upper = pre[:, 1, :]
        sig = jax.nn.sigmoid(gate)
        act = gate * sig
        hidden = (act * upper).astype(jnp.bfloat16)
        expert_out = jnp.dot(hidden, second, preferred_element_type=jnp.float32).astype(jnp.bfloat16)
        grad_down = jnp.dot(hidden.T, pick_grad, preferred_element_type=jnp.float32).astype(jnp.bfloat16)
        grad_hidden = jnp.dot(pick_grad, second.T, preferred_element_type=jnp.float32)
        grad_gate = grad_hidden * upper * sig * (1.0 + gate * (1.0 - sig))
        grad_upper = grad_hidden * act
        grad_pre = jnp.stack([grad_gate, grad_upper], axis=1).astype(jnp.bfloat16).reshape(slots, 2 * HID)
        grad_first = jnp.dot(rows_in.T, grad_pre, preferred_element_type=jnp.float32).astype(jnp.bfloat16)
        pick_dx = jnp.dot(grad_pre, first_flat.T, preferred_element_type=jnp.float32).astype(jnp.bfloat16)
        out_sum = out_sum.at[token_index].add(weight[:, None] * expert_out.astype(jnp.float32))
        mask = jnp.where(valid, jnp.float32(1.0), jnp.float32(0.0))
        grad_sum = grad_sum.at[token_index].add(mask[:, None] * pick_dx.astype(jnp.float32))
        return (out_sum, grad_sum), (grad_first.reshape(D, 2, HID), grad_down)

    start = (jnp.zeros((TOKENS, D), jnp.float32), jnp.zeros((TOKENS, D), jnp.float32))
    (out_sum, grad_sum), (grad_first, grad_second) = lax.scan(one_expert, start, jnp.arange(EXPERTS, dtype=jnp.int32))
    return out_sum.astype(jnp.bfloat16), grad_sum.astype(jnp.bfloat16), grad_first, grad_second
```

```python
import functools

import jax
import jax.numpy as jnp
import numpy as np
from jax import lax
from jax.experimental import pallas as pl
from jax.experimental.pallas import tpu as pltpu
from jax.sharding import PartitionSpec as P

CAP = 24
BLK = 2 * CAP
GROUPS = 4
MSG = jnp.float32
MESH = pl.DeviceIdType.MESH
BF = jnp.bfloat16
F32 = jnp.float32


def dot(a, b, ca, cb):
    return lax.dot_general(a, b, (((ca,), (cb,)), ((), ())), preferred_element_type=F32)


def landed(ref, sem):
    pltpu.make_async_copy(ref, ref, sem).wait()


def kernel(
    ne, nz, routes, scores, tokens, ograd, wgu, wd, slot, lower,
    out, gtok, ggu, gdn,
    place, whi, wlo, disp, rbuf, rows, grads, wgu2, wdp, part,
    s_up, r_up, s_dn, r_dn, hid, gp, xo_s, xo_r, own, cb_s, cb_r, tg_u, tg_d,
    d_send, d_recv, w_send, w_recv, f_send, f_recv,
    ru_send, ru_recv, rd_send, rd_recv, gu_send, gu_recv, gd_send, gd_recv,
    o_send, o_recv, c_send, c_recv, t_send, t_recv,
):
    e = lax.axis_index("expert")
    dp = lax.axis_index("dp")
    b = dp // nz
    z = lax.rem(dp, nz)
    side = (1 - b) * nz + z
    above = b * nz + lax.rem(z + 1, nz)
    below = b * nz + lax.rem(z + nz - 1, nz)
    slots = ne * CAP
    width = tokens.shape[1]
    half = wd.shape[1]
    share = slots // nz
    n_up, n_dn = nz // 2, nz // 2 - 1
    chunks = [(0, 2 * half), (2 * half, 3 * half)]
    per = ne // GROUPS

    def far(src, dst, send, recv, to_e, to_dp):
        return pltpu.make_async_remote_copy(
            src_ref=src, dst_ref=dst, send_sem=send, recv_sem=recv,
            device_id=(to_e, to_dp), device_id_type=MESH,
        )

    barrier = pltpu.get_barrier_semaphore()

    def greet(i, c):
        pl.semaphore_signal(
            barrier, inc=1, device_id=(lax.rem(e + i, ne), dp), device_id_type=MESH
        )
        return c

    lax.fori_loop(1, ne, greet, 0)
    for to in (side, above, below):
        pl.semaphore_signal(barrier, inc=1, device_id=(e, to), device_id_type=MESH)

    combine = scores[...] / jnp.sum(scores[...], axis=1, keepdims=True)
    slot_e, slot_r = slot[0:1, :], slot[1:2, :]
    tok = tokens.shape[0]
    hit = jnp.zeros((tok, slots), F32)
    weight = jnp.zeros((tok, slots), F32)
    for j in range(routes.shape[1]):
        named = routes[:, j : j + 1] == slot_e
        hit = jnp.where(named, 1.0, hit)
        weight = jnp.where(named, combine[:, j : j + 1], weight)
    rank = dot(lower[...], hit.astype(BF), 1, 0)
    taken = jnp.where(rank == slot_r.astype(F32), hit, 0.0)
    weight = weight * taken
    place[...] = taken.astype(BF)
    high = weight.astype(BF)
    whi[...] = high
    wlo[...] = (weight - high.astype(F32)).astype(BF)
    send_rows = dot(place[...], tokens[...], 0, 0)
    send_grad = dot(whi[...], ograd[...], 0, 0) + dot(wlo[...], ograd[...], 0, 0)
    both = jnp.concatenate(
        [send_rows.reshape(ne, CAP, width), send_grad.reshape(ne, CAP, width)], axis=1
    )
    disp[...] = both.reshape(ne * BLK, width).astype(BF)
    pl.semaphore_wait(barrier, ne + 2)

    def block(i):
        return pl.ds(pl.multiple_of(i * BLK, BLK), BLK)

    def dispatch(i, c):
        to = lax.rem(e + i, ne)
        far(disp.at[block(to)], rbuf.at[0, block(e)], d_send, d_recv.at[e // per], to, dp).start()
        return c

    lax.fori_loop(1, ne, dispatch, 0)
    pltpu.make_async_copy(disp.at[block(e)], rbuf.at[0, block(e)], d_recv.at[e // per]).start()

    w1 = far(wgu.at[1 - b], wgu2.at[pl.ds(width, width)], w_send.at[0], w_recv.at[0], e, side)
    w2 = far(wd.at[1 - b], wdp, w_send.at[1], w_recv.at[1], e, side)
    w1.start()
    w2.start()
    wgu2[0:width, :] = wgu[b]

    grp = per * BLK
    forward = []
    for g in range(GROUPS):
        at = pl.ds(g * grp, grp)
        landed(rbuf.at[0, at], d_recv.at[g])
        move = far(rbuf.at[0, at], rbuf.at[1, at], f_send.at[g], f_recv.at[g], e, side)
        move.start()
        forward.append(move)

    def unpack(which):
        got = rbuf[which].astype(F32).reshape(ne, BLK, width)
        cols = slice(which * width, (which + 1) * width)
        rows[:, cols] = got[:, :CAP].reshape(slots, width).astype(BF)
        grads[:, cols] = got[:, CAP:].reshape(slots, width).astype(BF)

    unpack(0)
    w1.wait_recv()
    w2.wait_recv()
    for move in forward:
        move.wait_recv()
    unpack(1)

    step = slots // 4
    wd2 = jnp.concatenate([wd[b], wdp[...]], axis=1)

    def partial(i, c):
        at = pl.ds(pl.multiple_of(i * step, step), step)
        part[at, 0 : 2 * half] = dot(rows[at, :], wgu2[...], 1, 0)
        part[at, 2 * half : 3 * half] = dot(grads[at, :], wd2, 1, 1)
        return c

    lax.fori_loop(0, 4, partial, 0)

    def of(d):
        return pl.ds(pl.multiple_of(d * share, share), share)

    def sum_up(k, first):
        d = lax.rem(z + n_up - k, nz)
        for c, (lo, hi) in enumerate(chunks):
            value = part[of(d), lo:hi]
            if not first:
                landed(r_up.at[k - 1, :, lo:hi], ru_recv.at[k - 1, c])
                value = value + r_up[k - 1, :, lo:hi].astype(F32)
            s_up[k, :, lo:hi] = value.astype(MSG)
            far(
                s_up.at[k, :, lo:hi], r_up.at[k, :, lo:hi],
                ru_send.at[k, c], ru_recv.at[k, c], e, above,
            ).start()

    def sum_dn(k, first):
        d = lax.rem(z + nz - n_dn + k, nz)
        for c, (lo, hi) in enumerate(chunks):
            value = part[of(d), lo:hi]
            if not first:
                landed(r_dn.at[k - 1, :, lo:hi], rd_recv.at[k - 1, c])
                value = value + r_dn[k - 1, :, lo:hi].astype(F32)
            s_dn[k, :, lo:hi] = value.astype(MSG)
            far(
                s_dn.at[k, :, lo:hi], r_dn.at[k, :, lo:hi],
                rd_send.at[k, c], rd_recv.at[k, c], e, below,
            ).start()

    sum_up(0, True)
    sum_dn(0, True)

    def hop(k, c):
        sum_up(k, False)
        sum_dn(k, False)
        return c

    lax.fori_loop(1, n_dn, hop, 0)
    sum_up(n_up - 1, False)
    total = []
    for c, (lo, hi) in enumerate(chunks):
        landed(r_dn.at[n_dn - 1, :, lo:hi], rd_recv.at[n_dn - 1, c])
        landed(r_up.at[n_up - 1, :, lo:hi], ru_recv.at[n_up - 1, c])
        total.append(
            part[of(z), lo:hi]
            + r_up[n_up - 1, :, lo:hi].astype(F32)
            + r_dn[n_dn - 1, :, lo:hi].astype(F32)
        )
    gate, upper, grad_hidden = total[0][:, :half], total[0][:, half:], total[1]
    sig = jax.nn.sigmoid(gate)
    act = gate * sig
    hid[of(z), :] = (act * upper).astype(BF)
    gp[of(z), 0:half] = (grad_hidden * upper * sig * (1.0 + gate * (1.0 - sig))).astype(BF)
    gp[of(z), half : 2 * half] = (grad_hidden * act).astype(BF)

    def pass_on(k, first, way):
        d = lax.rem(z + nz - k, nz) if way else lax.rem(z + k, nz)
        send, recv, to = (gu_send, gu_recv, above) if way else (gd_send, gd_recv, below)
        for c, ref in enumerate((hid, gp)):
            if not first:
                landed(ref.at[of(d)], recv.at[k - 1, c])
            far(ref.at[of(d)], ref.at[of(d)], send.at[k, c], recv.at[k, c], e, to).start()

    pass_on(0, True, True)
    pass_on(0, True, False)

    def relay(k, c):
        pass_on(k, False, True)
        pass_on(k, False, False)
        return c

    lax.fori_loop(1, n_dn, relay, 0)
    pass_on(n_up - 1, False, True)
    for c, ref in enumerate((hid, gp)):
        landed(ref.at[of(lax.rem(z + n_dn, nz))], gd_recv.at[n_dn - 1, c])
        landed(ref.at[of(lax.rem(z + nz - n_up, nz))], gu_recv.at[n_up - 1, c])

    def spread(i, c):
        at = pl.ds(pl.multiple_of(i * step, step), step)
        eo = dot(hid[at, :], wd2, 1, 0)
        own[0, at, :] = eo[:, :width]
        xo_s[0, at, :] = eo[:, width:].astype(BF)
        dx = dot(gp[at, :], wgu2[...], 1, 1)
        own[1, at, :] = dx[:, :width]
        xo_s[1, at, :] = dx[:, width:].astype(BF)
        return c

    lax.fori_loop(0, 4, spread, 0)
    cross = []
    for i in range(2):
        move = far(xo_s.at[i], xo_r.at[i], o_send.at[i], o_recv.at[i], e, side)
        move.start()
        cross.append(move)
    gg = dot(rows[...], gp[...], 0, 0)
    tg_u[...] = gg[width:].astype(BF)
    t1 = far(tg_u, ggu.at[b], t_send.at[0], t_recv.at[0], e, side)
    t1.start()
    ggu[b] = gg[:width].astype(BF)
    gd = dot(hid[...], grads[...], 0, 0)
    tg_d[...] = gd[:, width:].astype(BF)
    t2 = far(tg_d, gdn.at[b], t_send.at[1], t_recv.at[1], e, side)
    t2.start()
    gdn[b] = gd[:, :width].astype(BF)

    for move in cross:
        move.wait_recv()
    back = [
        (own[i] + xo_r[i].astype(F32)).reshape(ne, CAP, width) for i in range(2)
    ]
    cb_s[...] = jnp.concatenate(back, axis=1).reshape(ne * BLK, width).astype(BF)

    def give_back(i, c):
        to = lax.rem(e + i, ne)
        far(cb_s.at[block(to)], cb_r.at[block(e)], c_send, c_recv, to, dp).start()
        return c

    lax.fori_loop(1, ne, give_back, 0)
    pltpu.make_async_copy(cb_s.at[block(e)], cb_r.at[block(e)], c_recv).start()
    landed(cb_r, c_recv)
    got = cb_r[...].astype(F32).reshape(ne, BLK, width)
    eo = got[:, :CAP].reshape(slots, width).astype(BF)
    dx = got[:, CAP:].reshape(slots, width).astype(BF)
    out[...] = (dot(whi[...], eo, 1, 0) + dot(wlo[...], eo, 1, 0)).astype(BF)
    gtok[...] = dot(place[...], dx, 1, 0).astype(BF)

    t1.wait_recv()
    t2.wait_recv()
    sent = pl.ds(0, (ne - 1) * BLK)
    landed(disp.at[sent], d_send)
    landed(cb_s.at[sent], c_send)
    for move in (w1, w2, *forward, *cross, t1, t2):
        move.wait_send()
    for send, ring, n in ((ru_send, s_up, n_up), (rd_send, s_dn, n_dn)):
        for k in range(n):
            for c, (lo, hi) in enumerate(chunks):
                landed(ring.at[k, :, lo:hi], send.at[k, c])
    for send, n in ((gu_send, n_up), (gd_send, n_dn)):
        for k in range(n):
            for c, ref in enumerate((hid, gp)):
                landed(ref.at[pl.ds(0, share)], send.at[k, c])


def body(tokens, out_grad, routes, scores, w_gate_up, w_down):
    ne, ndp = lax.axis_size("expert"), lax.axis_size("dp")
    nz = ndp // 2
    tok, width = tokens.shape
    hidden = w_down.shape[1]
    half = hidden // 2
    slots = ne * CAP
    share = slots // nz
    n_up, n_dn = nz // 2, nz // 2 - 1
    ids = np.arange(slots)
    slot = jnp.asarray(np.stack([ids // CAP, ids % CAP]).astype(np.int32))
    lower = jnp.asarray(np.tril(np.ones((tok, tok), np.float32), -1)).astype(BF)
    wgu = w_gate_up[0].reshape(width, 2, 2, half).transpose(2, 0, 1, 3).reshape(2, width, 2 * half)
    wd = w_down[0].reshape(2, half, width)
    dma = pltpu.SemaphoreType.DMA
    out, gtok, ggu, gdn = pl.pallas_call(
        functools.partial(kernel, ne, nz),
        out_shape=(
            jax.ShapeDtypeStruct((tok, width), BF),
            jax.ShapeDtypeStruct((tok, width), BF),
            jax.ShapeDtypeStruct((2, width, 2 * half), BF),
            jax.ShapeDtypeStruct((2, half, width), BF),
        ),
        in_specs=[pl.BlockSpec(memory_space=pltpu.VMEM)] * 8,
        out_specs=[pl.BlockSpec(memory_space=pltpu.VMEM)] * 4,
        scratch_shapes=[
            pltpu.VMEM((tok, slots), BF),
            pltpu.VMEM((tok, slots), BF),
            pltpu.VMEM((tok, slots), BF),
            pltpu.VMEM((ne * BLK, width), BF),
            pltpu.VMEM((2, ne * BLK, width), BF),
            pltpu.VMEM((slots, 2 * width), BF),
            pltpu.VMEM((slots, 2 * width), BF),
            pltpu.VMEM((2 * width, 2 * half), BF),
            pltpu.VMEM((half, width), BF),
            pltpu.VMEM((slots, 3 * half), F32),
            pltpu.VMEM((n_up, share, 3 * half), MSG),
            pltpu.VMEM((n_up, share, 3 * half), MSG),
            pltpu.VMEM((n_dn, share, 3 * half), MSG),
            pltpu.VMEM((n_dn, share, 3 * half), MSG),
            pltpu.VMEM((slots, half), BF),
            pltpu.VMEM((slots, 2 * half), BF),
            pltpu.VMEM((2, slots, width), BF),
            pltpu.VMEM((2, slots, width), BF),
            pltpu.VMEM((2, slots, width), F32),
            pltpu.VMEM((ne * BLK, width), BF),
            pltpu.VMEM((ne * BLK, width), BF),
            pltpu.VMEM((width, 2 * half), BF),
            pltpu.VMEM((half, width), BF),
            dma, dma((GROUPS,)),
            dma((2,)), dma((2,)),
            dma((GROUPS,)), dma((GROUPS,)),
            dma((n_up, 2)), dma((n_up, 2)), dma((n_dn, 2)), dma((n_dn, 2)),
            dma((n_up, 2)), dma((n_up, 2)), dma((n_dn, 2)), dma((n_dn, 2)),
            dma((2,)), dma((2,)),
            dma, dma,
            dma((2,)), dma((2,)),
        ],
        compiler_params=pltpu.CompilerParams(
            collective_id=0, has_side_effects=True, vmem_limit_bytes=48 * 1024 * 1024
        ),
    )(routes, scores, tokens, out_grad, wgu, wd, slot, lower)
    grad_first = (
        ggu.reshape(2, width, 2, half).transpose(1, 2, 0, 3).reshape(1, width, 2, hidden)
    )
    return out, gtok, grad_first, gdn.reshape(1, hidden, width)


def solution(mesh):
    placed = (
        P("expert", "dp"),
        P("expert", "dp"),
        P("expert", None),
        P("expert", None),
        P("expert", "dp", None, None),
        P("expert", None, "dp"),
    )
    return jax.shard_map(
        body,
        mesh=mesh,
        in_specs=placed,
        out_specs=(
            P("expert", "dp"),
            P("expert", "dp"),
            P("expert", "dp", None, None),
            P("expert", None, "dp"),
        ),
        check_vma=False,
    )
```

```python
import functools

import jax
import jax.numpy as jnp
import numpy as np
from jax import lax
from jax.experimental import pallas as pl
from jax.experimental.pallas import tpu as pltpu
from jax.sharding import PartitionSpec as P

CAP = 24
BLK = 2 * CAP
GROUPS = 8
WIDE = 2
MESH = pl.DeviceIdType.MESH
BF = jnp.bfloat16
F32 = jnp.float32


def dot(a, b, ca, cb):
    return lax.dot_general(a, b, (((ca,), (cb,)), ((), ())), preferred_element_type=F32)


def landed(ref, sem):
    pltpu.make_async_copy(ref, ref, sem).wait()


def kernel(
    ne, nz, routes, scores, tokens, ograd, wgu, wd, slot, lower,
    out, gtok, ggu, gdn,
    place, whi, wlo, disp, rbuf, rows, grads, wgu2, wdp, part,
    su_n, ru_n, su_w, ru_w, sd_n, rd_n, sd_w, rd_w,
    act, xo_s, xo_r, own, cb_s, cb_r, tg_u, tg_d, acc_u, acc_d,
    d_send, d_recv, w_send, w_recv, f_send, f_recv,
    ru_send, ru_recv, rd_send, rd_recv, gu_send, gu_recv, gd_send, gd_recv,
    o_send, o_recv, c_send, c_recv, t_send, t_recv,
):
    e = lax.axis_index("expert")
    dp = lax.axis_index("dp")
    b = dp // nz
    z = lax.rem(dp, nz)
    side = (1 - b) * nz + z
    above = b * nz + lax.rem(z + 1, nz)
    below = b * nz + lax.rem(z + nz - 1, nz)
    slots = ne * CAP
    width = tokens.shape[1]
    half = wd.shape[1]
    share = slots // nz
    n_up, n_dn = nz // 2, nz // 2 - 1
    narrow = max(1, n_up - WIDE)
    per = ne // GROUPS

    def far(src, dst, send, recv, to_e, to_dp):
        return pltpu.make_async_remote_copy(
            src_ref=src, dst_ref=dst, send_sem=send, recv_sem=recv,
            device_id=(to_e, to_dp), device_id_type=MESH,
        )

    barrier = pltpu.get_barrier_semaphore()

    def greet(i, c):
        pl.semaphore_signal(
            barrier, inc=1, device_id=(lax.rem(e + i, ne), dp), device_id_type=MESH
        )
        return c

    lax.fori_loop(1, ne, greet, 0)
    for to in (side, above, below):
        pl.semaphore_signal(barrier, inc=1, device_id=(e, to), device_id_type=MESH)

    combine = scores[...] / jnp.sum(scores[...], axis=1, keepdims=True)
    slot_e, slot_r = slot[0:1, :], slot[1:2, :]
    tok = tokens.shape[0]
    hit = jnp.zeros((tok, slots), F32)
    weight = jnp.zeros((tok, slots), F32)
    for j in range(routes.shape[1]):
        named = routes[:, j : j + 1] == slot_e
        hit = jnp.where(named, 1.0, hit)
        weight = jnp.where(named, combine[:, j : j + 1], weight)
    rank = dot(lower[...], hit.astype(BF), 1, 0)
    taken = jnp.where(rank == slot_r.astype(F32), hit, 0.0)
    weight = weight * taken
    place[...] = taken.astype(BF)
    high = weight.astype(BF)
    whi[...] = high
    wlo[...] = (weight - high.astype(F32)).astype(BF)

    send_rows = dot(place[...], tokens[...], 0, 0).reshape(ne, CAP, width)
    send_grad = dot(whi[...], ograd[...], 0, 0) + dot(wlo[...], ograd[...], 0, 0)
    both = jnp.concatenate([send_rows, send_grad.reshape(ne, CAP, width)], axis=1)
    disp[...] = both.reshape(ne * BLK, width).astype(BF)
    pl.semaphore_wait(barrier, ne + 2)

    def block(i):
        return pl.ds(pl.multiple_of(i * BLK, BLK), BLK)

    def dispatch(i, c):
        to = lax.rem(e + i, ne)
        far(
            disp.at[block(to)], rbuf.at[0, block(i)], d_send, d_recv.at[i // per], to, dp
        ).start()
        return c

    lax.fori_loop(1, ne, dispatch, 0)
    pltpu.make_async_copy(disp.at[block(e)], rbuf.at[0, block(0)], d_recv.at[0]).start()

    w1 = far(wgu.at[1 - b], wgu2.at[pl.ds(width, width)], w_send.at[0], w_recv.at[0], e, side)
    w2 = far(wd.at[1 - b], wdp, w_send.at[1], w_recv.at[1], e, side)
    w1.start()
    w2.start()
    wgu2[0:width, :] = wgu[b]
    moves = []
    for g in range(GROUPS):
        at = pl.ds(g * per * BLK, per * BLK)
        landed(rbuf.at[0, at], d_recv.at[g])
        move = far(rbuf.at[0, at], rbuf.at[1, at], f_send.at[g], f_recv.at[g], e, side)
        move.start()
        moves.append(move)

    def unpack(which):
        got = rbuf[which].astype(F32).reshape(ne, BLK, width)
        cols = slice(which * width, (which + 1) * width)
        rows[:, cols] = got[:, :CAP].reshape(slots, width).astype(BF)
        grads[:, cols] = got[:, CAP:].reshape(slots, width).astype(BF)

    unpack(0)
    w1.wait_recv()
    w2.wait_recv()
    for move in moves:
        move.wait_recv()
    unpack(1)

    step = slots // 4
    wd2 = jnp.concatenate([wd[b], wdp[...]], axis=1)

    def partial(i, c):
        at = pl.ds(pl.multiple_of(i * step, step), step)
        value = dot(rows[at, :], wgu2[...], 1, 0)
        part[0, at, :] = value[:, :half]
        part[1, at, :] = value[:, half:]
        part[2, at, :] = dot(grads[at, :], wd2, 1, 1)
        return c

    lax.fori_loop(0, 4, partial, 0)

    def of(d):
        return pl.ds(pl.multiple_of(d * share, share), share)

    def sums(up, k, c):
        n = n_up if up else n_dn
        if k < 0 or k >= n:
            return
        d = lax.rem(z + n_up - k, nz) if up else lax.rem(z + nz - n_dn + k, nz)
        send, recv = (ru_send, ru_recv) if up else (rd_send, rd_recv)
        value = part[c, of(d), :]
        if k:
            value = value + arrived(up, k - 1, c)
        if k < narrow:
            src, dst, at = (su_n, ru_n, k) if up else (sd_n, rd_n, k)
        else:
            src, dst, at = (su_w, ru_w, k - narrow) if up else (sd_w, rd_w, k - narrow)
        src[c, at] = value.astype(src.dtype)
        far(
            src.at[c, at], dst.at[c, at], send.at[c, k], recv.at[c, k],
            e, above if up else below,
        ).start()

    def arrived(up, k, c):
        if k < narrow:
            ref, at = (ru_n if up else rd_n), k
        else:
            ref, at = (ru_w if up else rd_w), k - narrow
        landed(ref.at[c, at], (ru_recv if up else rd_recv).at[c, k])
        return ref[c, at].astype(F32)

    def summed(c):
        return part[c, of(z), :] + arrived(False, n_dn - 1, c) + arrived(True, n_up - 1, c)

    def gathers(up, k, c):
        n = n_up if up else n_dn
        if k < 0 or k > n:
            return
        d = lax.rem(z + nz - k, nz) if up else lax.rem(z + k, nz)
        send, recv = (gu_send, gu_recv) if up else (gd_send, gd_recv)
        at = act.at[c, of(d)]
        if k:
            landed(at, recv.at[c, k - 1])
        if k < n:
            far(at, at, send.at[c, k], recv.at[c, k], e, above if up else below).start()

    def finish(d, first):
        hid = act[0, of(d), :]
        both = jnp.concatenate([act[1, of(d), :], act[2, of(d), :]], axis=1)
        eo = dot(hid, jnp.concatenate([wd[b], wdp[...]], axis=1), 1, 0)
        dx = dot(both, wgu2[...], 1, 1)
        own[0, of(d), :] = eo[:, :width]
        own[1, of(d), :] = dx[:, :width]
        xo_s[d] = jnp.concatenate([eo[:, width:], dx[:, width:]], axis=0).astype(BF)
        far(xo_s.at[d], xo_r.at[d], o_send.at[d], o_recv.at[d], e, side).start()
        to_u = dot(rows[of(d), :], both, 0, 0)
        to_d = dot(hid, grads[of(d), :], 0, 0)
        acc_u[...] = to_u if first else acc_u[...] + to_u
        acc_d[...] = to_d if first else acc_d[...] + to_d

    n_blk = share // CAP

    def deliver(d):
        landed(xo_r.at[d], o_recv.at[d])
        got = xo_r[d].astype(F32)
        eo = (own[0, of(d), :] + got[:share]).reshape(n_blk, CAP, width)
        dx = (own[1, of(d), :] + got[share:]).reshape(n_blk, CAP, width)
        whole = jnp.concatenate([eo, dx], axis=1).reshape(n_blk * BLK, width)
        cb_s[pl.ds(pl.multiple_of(d * n_blk * BLK, n_blk * BLK), n_blk * BLK), :] = whole.astype(BF)
        for i in range(n_blk):
            p = d * n_blk + i
            to = lax.rem(e + ne - p, ne)

            @pl.when(p != 0)
            def _():
                far(cb_s.at[block(p)], cb_r.at[block(e)], c_send, c_recv, to, dp).start()

            @pl.when(p == 0)
            def _():
                pltpu.make_async_copy(cb_s.at[block(p)], cb_r.at[block(e)], c_recv).start()

    def at_step(k):
        if k == 0:
            return [z]
        if k > n_dn:
            return [lax.rem(z + nz - k, nz)]
        return [lax.rem(z + nz - k, nz), lax.rem(z + k, nz)]

    for k in range(n_up):
        for c in range(3):
            sums(True, k, c)
            sums(False, k, c)
    gate, upper, grad_hidden = summed(0), summed(1), summed(2)
    sig = jax.nn.sigmoid(gate)
    act[0, of(z), :] = (gate * sig * upper).astype(BF)
    act[1, of(z), :] = (grad_hidden * upper * sig * (1.0 + gate * (1.0 - sig))).astype(BF)
    act[2, of(z), :] = (grad_hidden * (gate * sig)).astype(BF)
    for k in range(n_up + 1):
        for c in range(3):
            gathers(True, k, c)
            gathers(False, k, c)
        for d in at_step(k):
            finish(d, k == 0)
        if k == n_up:
            tg_u[...] = acc_u[width:, :].astype(BF)
            t1 = far(tg_u, ggu.at[b], t_send.at[0], t_recv.at[0], e, side)
            t1.start()
            tg_d[...] = acc_d[:, width:].astype(BF)
            t2 = far(tg_d, gdn.at[b], t_send.at[1], t_recv.at[1], e, side)
            t2.start()
        if k:
            for d in at_step(k - 1):
                deliver(d)
    for d in at_step(n_up):
        deliver(d)
    ggu[b] = acc_u[:width, :].astype(BF)
    gdn[b] = acc_d[:, :width].astype(BF)

    landed(cb_r, c_recv)
    got = cb_r[...].astype(F32).reshape(ne, BLK, width)
    eo = got[:, :CAP].reshape(slots, width).astype(BF)
    dx = got[:, CAP:].reshape(slots, width).astype(BF)
    out[...] = (dot(whi[...], eo, 1, 0) + dot(wlo[...], eo, 1, 0)).astype(BF)
    gtok[...] = dot(place[...], dx, 1, 0).astype(BF)

    t1.wait_recv()
    t2.wait_recv()
    landed(disp.at[pl.ds(0, (ne - 1) * BLK)], d_send)
    landed(cb_s.at[pl.ds(0, (ne - 1) * BLK)], c_send)
    for move in (w1, w2, *moves, t1, t2):
        move.wait_send()
    for d in range(nz):
        landed(xo_s.at[d], o_send.at[d])
    for up, n in ((True, n_up), (False, n_dn)):
        for k in range(n):
            for c in range(3):
                if k < narrow:
                    src, at = (su_n if up else sd_n), k
                else:
                    src, at = (su_w if up else sd_w), k - narrow
                landed(src.at[c, at], (ru_send if up else rd_send).at[c, k])
                landed(act.at[c, pl.ds(0, share)], (gu_send if up else gd_send).at[c, k])


def body(tokens, out_grad, routes, scores, w_gate_up, w_down):
    ne, ndp = lax.axis_size("expert"), lax.axis_size("dp")
    nz = ndp // 2
    tok, width = tokens.shape
    hidden = w_down.shape[1]
    half = hidden // 2
    slots = ne * CAP
    share = slots // nz
    n_up, n_dn = nz // 2, nz // 2 - 1
    narrow = max(1, n_up - WIDE)
    ids = np.arange(slots)
    slot = jnp.asarray(np.stack([ids // CAP, ids % CAP]).astype(np.int32))
    lower = jnp.asarray(np.tril(np.ones((tok, tok), np.float32), -1)).astype(BF)
    wgu = w_gate_up[0].reshape(width, 2, 2, half).transpose(2, 0, 1, 3).reshape(2, width, 2 * half)
    wd = w_down[0].reshape(2, half, width)
    dma = pltpu.SemaphoreType.DMA
    ups = [pltpu.VMEM((3, narrow, share, half), BF)] * 2
    ups += [pltpu.VMEM((3, n_up - narrow, share, half), F32)] * 2
    dns = [pltpu.VMEM((3, narrow, share, half), BF)] * 2
    dns += [pltpu.VMEM((3, max(1, n_dn - narrow), share, half), F32)] * 2
    out, gtok, ggu, gdn = pl.pallas_call(
        functools.partial(kernel, ne, nz),
        out_shape=(
            jax.ShapeDtypeStruct((tok, width), BF),
            jax.ShapeDtypeStruct((tok, width), BF),
            jax.ShapeDtypeStruct((2, width, 2 * half), BF),
            jax.ShapeDtypeStruct((2, half, width), BF),
        ),
        in_specs=[pl.BlockSpec(memory_space=pltpu.VMEM)] * 8,
        out_specs=[pl.BlockSpec(memory_space=pltpu.VMEM)] * 4,
        scratch_shapes=[
            pltpu.VMEM((tok, slots), BF),
            pltpu.VMEM((tok, slots), BF),
            pltpu.VMEM((tok, slots), BF),
            pltpu.VMEM((ne * BLK, width), BF),
            pltpu.VMEM((2, ne * BLK, width), BF),
            pltpu.VMEM((slots, 2 * width), BF),
            pltpu.VMEM((slots, 2 * width), BF),
            pltpu.VMEM((2 * width, 2 * half), BF),
            pltpu.VMEM((half, width), BF),
            pltpu.VMEM((3, slots, half), F32),
            *ups,
            *dns,
            pltpu.VMEM((3, slots, half), BF),
            pltpu.VMEM((nz, 2 * share, width), BF),
            pltpu.VMEM((nz, 2 * share, width), BF),
            pltpu.VMEM((2, slots, width), F32),
            pltpu.VMEM((ne * BLK, width), BF),
            pltpu.VMEM((ne * BLK, width), BF),
            pltpu.VMEM((width, 2 * half), BF),
            pltpu.VMEM((half, width), BF),
            pltpu.VMEM((2 * width, 2 * half), F32),
            pltpu.VMEM((half, 2 * width), F32),
            dma, dma((GROUPS,)),
            dma((2,)), dma((2,)),
            dma((GROUPS,)), dma((GROUPS,)),
            dma((3, n_up)), dma((3, n_up)), dma((3, n_dn)), dma((3, n_dn)),
            dma((3, n_up)), dma((3, n_up)), dma((3, n_dn)), dma((3, n_dn)),
            dma((nz,)), dma((nz,)),
            dma, dma,
            dma((2,)), dma((2,)),
        ],
        compiler_params=pltpu.CompilerParams(
            collective_id=0, has_side_effects=True, vmem_limit_bytes=48 * 1024 * 1024
        ),
    )(routes, scores, tokens, out_grad, wgu, wd, slot, lower)
    grad_first = (
        ggu.reshape(2, width, 2, half).transpose(1, 2, 0, 3).reshape(1, width, 2, hidden)
    )
    return out, gtok, grad_first, gdn.reshape(1, hidden, width)


def solution(mesh):
    placed = (
        P("expert", "dp"),
        P("expert", "dp"),
        P("expert", None),
        P("expert", None),
        P("expert", "dp", None, None),
        P("expert", None, "dp"),
    )
    return jax.shard_map(
        body,
        mesh=mesh,
        in_specs=placed,
        out_specs=(
            P("expert", "dp"),
            P("expert", "dp"),
            P("expert", "dp", None, None),
            P("expert", None, "dp"),
        ),
        check_vma=False,
    )
```

```python
import functools

import jax
import jax.numpy as jnp
import numpy as np
from jax import lax
from jax.experimental import pallas as pl
from jax.experimental.pallas import tpu as pltpu
from jax.sharding import PartitionSpec as P

CAP = 24
BLK = 2 * CAP
GROUPS = 8
WIDE = 3
MESH = pl.DeviceIdType.MESH
BF = jnp.bfloat16
F32 = jnp.float32


def dot(a, b, ca, cb):
    return lax.dot_general(a, b, (((ca,), (cb,)), ((), ())), preferred_element_type=F32)


def landed(ref, sem):
    pltpu.make_async_copy(ref, ref, sem).wait()


def kernel(
    ne, nz, routes, scores, tokens, ograd, wgu, wd, slot, lower,
    out, gtok, ggu, gdn,
    place, whi, wlo, disp, rbuf, rows, grads, wgu2, wdp, part,
    su_n, ru_n, su_w, ru_w, sd_n, rd_n, sd_w, rd_w,
    act, xo_s, xo_r, own, cb_s, cb_r, tg_u, tg_d, acc_u, acc_d,
    d_send, d_recv, w_send, w_recv, f_send, f_recv,
    ru_send, ru_recv, rd_send, rd_recv, gu_send, gu_recv, gd_send, gd_recv,
    o_send, o_recv, c_send, c_recv, t_send, t_recv,
):
    e = lax.axis_index("expert")
    dp = lax.axis_index("dp")
    b = dp // nz
    z = lax.rem(dp, nz)
    side = (1 - b) * nz + z
    above = b * nz + lax.rem(z + 1, nz)
    below = b * nz + lax.rem(z + nz - 1, nz)
    slots = ne * CAP
    width = tokens.shape[1]
    half = wd.shape[1]
    share = slots // nz
    n_up, n_dn = nz // 2, nz // 2 - 1
    narrow = max(1, n_up - WIDE)
    per = ne // GROUPS
    mid = ne // 2

    def partner(i):
        to = lax.rem(e // mid + i // mid, 2) * mid + lax.rem(e + i, mid)
        return to, lax.rem(b + i // mid, 2) * nz + z

    def sender(i):
        to = lax.rem(e // mid + i // mid, 2) * mid + lax.rem(e + ne - i, mid)
        return to, lax.rem(b + i // mid, 2) * nz + z

    def far(src, dst, send, recv, to_e, to_dp):
        return pltpu.make_async_remote_copy(
            src_ref=src, dst_ref=dst, send_sem=send, recv_sem=recv,
            device_id=(to_e, to_dp), device_id_type=MESH,
        )

    barrier = pltpu.get_barrier_semaphore()

    def greet(i, c):
        pl.semaphore_signal(barrier, inc=1, device_id=partner(i), device_id_type=MESH)
        return c

    lax.fori_loop(1, ne, greet, 0)
    for to in (side, above, below):
        pl.semaphore_signal(barrier, inc=1, device_id=(e, to), device_id_type=MESH)

    combine = scores[...] / jnp.sum(scores[...], axis=1, keepdims=True)
    slot_e, slot_r = slot[0:1, :], slot[1:2, :]
    tok = tokens.shape[0]
    hit = jnp.zeros((tok, slots), F32)
    weight = jnp.zeros((tok, slots), F32)
    for j in range(routes.shape[1]):
        named = routes[:, j : j + 1] == slot_e
        hit = jnp.where(named, 1.0, hit)
        weight = jnp.where(named, combine[:, j : j + 1], weight)
    rank = dot(lower[...], hit.astype(BF), 1, 0)
    taken = jnp.where(rank == slot_r.astype(F32), hit, 0.0)
    weight = weight * taken
    place[...] = taken.astype(BF)
    high = weight.astype(BF)
    whi[...] = high
    wlo[...] = (weight - high.astype(F32)).astype(BF)

    send_rows = dot(place[...], tokens[...], 0, 0).reshape(ne, CAP, width)
    send_grad = dot(whi[...], ograd[...], 0, 0) + dot(wlo[...], ograd[...], 0, 0)
    both = jnp.concatenate([send_rows, send_grad.reshape(ne, CAP, width)], axis=1)
    disp[...] = both.reshape(ne * BLK, width).astype(BF)
    pl.semaphore_wait(barrier, ne + 2)

    def block(i):
        return pl.ds(pl.multiple_of(i * BLK, BLK), BLK)

    def dispatch(i, c):
        to, col = partner(i)
        far(
            disp.at[block(to)], rbuf.at[i // mid, block(i)], d_send, d_recv.at[i // per], to, col
        ).start()
        return c

    lax.fori_loop(1, ne, dispatch, 0)
    pltpu.make_async_copy(disp.at[block(e)], rbuf.at[0, block(0)], d_recv.at[0]).start()

    w1 = far(wgu.at[1 - b], wgu2.at[pl.ds(width, width)], w_send.at[0], w_recv.at[0], e, side)
    w2 = far(wd.at[1 - b], wdp, w_send.at[1], w_recv.at[1], e, side)
    w1.start()
    w2.start()
    wgu2[0:width, :] = wgu[b]
    moves = []
    for g in range(GROUPS):
        at = pl.ds(g * per * BLK, per * BLK)
        part_of = g * per // mid
        here, there = rbuf.at[part_of, at], rbuf.at[1 - part_of, at]
        landed(here, d_recv.at[g])
        move = far(here, there, f_send.at[g], f_recv.at[g], e, side)
        move.start()
        moves.append(move)

    def unpack(which):
        got = rbuf[which].astype(F32).reshape(ne, BLK, width)
        cols = slice(which * width, (which + 1) * width)
        rows[:, cols] = got[:, :CAP].reshape(slots, width).astype(BF)
        grads[:, cols] = got[:, CAP:].reshape(slots, width).astype(BF)

    w1.wait_recv()
    w2.wait_recv()
    for move in moves:
        move.wait_recv()
    unpack(0)
    unpack(1)

    step = slots // 4
    wd2 = jnp.concatenate([wd[b], wdp[...]], axis=1)

    def partial(i, c):
        at = pl.ds(pl.multiple_of(i * step, step), step)
        value = dot(rows[at, :], wgu2[...], 1, 0)
        part[0, at, :] = value[:, :half]
        part[1, at, :] = value[:, half:]
        part[2, at, :] = dot(grads[at, :], wd2, 1, 1)
        return c

    lax.fori_loop(0, 4, partial, 0)

    def of(d):
        return pl.ds(pl.multiple_of(d * share, share), share)

    def sums(up, k, c):
        n = n_up if up else n_dn
        if k < 0 or k >= n:
            return
        d = lax.rem(z + n_up - k, nz) if up else lax.rem(z + nz - n_dn + k, nz)
        send, recv = (ru_send, ru_recv) if up else (rd_send, rd_recv)
        value = part[c, of(d), :]
        if k:
            value = value + arrived(up, k - 1, c)
        if k < narrow:
            src, dst, at = (su_n, ru_n, k) if up else (sd_n, rd_n, k)
        else:
            src, dst, at = (su_w, ru_w, k - narrow) if up else (sd_w, rd_w, k - narrow)
        src[c, at] = value.astype(src.dtype)
        far(
            src.at[c, at], dst.at[c, at], send.at[c, k], recv.at[c, k],
            e, above if up else below,
        ).start()

    def arrived(up, k, c):
        if k < narrow:
            ref, at = (ru_n if up else rd_n), k
        else:
            ref, at = (ru_w if up else rd_w), k - narrow
        landed(ref.at[c, at], (ru_recv if up else rd_recv).at[c, k])
        return ref[c, at].astype(F32)

    def summed(c):
        return part[c, of(z), :] + arrived(False, n_dn - 1, c) + arrived(True, n_up - 1, c)

    def gathers(up, k, c):
        n = n_up if up else n_dn
        if k < 0 or k > n:
            return
        d = lax.rem(z + nz - k, nz) if up else lax.rem(z + k, nz)
        send, recv = (gu_send, gu_recv) if up else (gd_send, gd_recv)
        at = act.at[c, of(d)]
        if k:
            landed(at, recv.at[c, k - 1])
        if k < n:
            far(at, at, send.at[c, k], recv.at[c, k], e, above if up else below).start()

    def finish(d, first):
        hid = act[0, of(d), :]
        both = jnp.concatenate([act[1, of(d), :], act[2, of(d), :]], axis=1)
        eo = dot(hid, jnp.concatenate([wd[b], wdp[...]], axis=1), 1, 0)
        dx = dot(both, wgu2[...], 1, 1)
        mine = jnp.concatenate([eo[:, :width], dx[:, :width]], axis=0)
        other = jnp.concatenate([eo[:, width:], dx[:, width:]], axis=0)

        @pl.when(d < nz // 2)
        def _():
            own[d] = mine
            xo_s[d] = other.astype(BF)

        @pl.when(d >= nz // 2)
        def _():
            own[d] = other
            xo_s[d] = mine.astype(BF)

        far(xo_s.at[d], xo_r.at[d], o_send.at[d], o_recv.at[d], e, side).start()
        to_u = dot(rows[of(d), :], both, 0, 0)
        to_d = dot(hid, grads[of(d), :], 0, 0)
        acc_u[...] = to_u if first else acc_u[...] + to_u
        acc_d[...] = to_d if first else acc_d[...] + to_d

    n_blk = share // CAP

    def deliver(d):
        landed(xo_r.at[d], o_recv.at[d])
        got = own[d] + xo_r[d].astype(F32)
        eo = got[:share].reshape(n_blk, CAP, width)
        dx = got[share:].reshape(n_blk, CAP, width)
        whole = jnp.concatenate([eo, dx], axis=1).reshape(n_blk * BLK, width)
        cb_s[pl.ds(pl.multiple_of(d * n_blk * BLK, n_blk * BLK), n_blk * BLK), :] = whole.astype(BF)
        for i in range(n_blk):
            p = d * n_blk + i
            to, col = sender(p)

            @pl.when(p != 0)
            def _():
                far(cb_s.at[block(p)], cb_r.at[block(e)], c_send, c_recv, to, col).start()

            @pl.when(p == 0)
            def _():
                pltpu.make_async_copy(cb_s.at[block(p)], cb_r.at[block(e)], c_recv).start()

    def at_step(k):
        if k == 0:
            return [z]
        if k > n_dn:
            return [lax.rem(z + nz - k, nz)]
        return [lax.rem(z + nz - k, nz), lax.rem(z + k, nz)]

    for k in range(n_up):
        for c in range(3):
            sums(True, k, c)
            sums(False, k, c)
    gate, upper, grad_hidden = summed(0), summed(1), summed(2)
    sig = jax.nn.sigmoid(gate)
    act[0, of(z), :] = (gate * sig * upper).astype(BF)
    act[1, of(z), :] = (grad_hidden * upper * sig * (1.0 + gate * (1.0 - sig))).astype(BF)
    act[2, of(z), :] = (grad_hidden * (gate * sig)).astype(BF)
    for k in range(n_up + 1):
        for c in range(3):
            gathers(True, k, c)
            gathers(False, k, c)
        for d in at_step(k):
            finish(d, k == 0)
        if k == n_up:
            tg_u[...] = acc_u[width:, :].astype(BF)
            t1 = far(tg_u, ggu.at[b], t_send.at[0], t_recv.at[0], e, side)
            t1.start()
            tg_d[...] = acc_d[:, width:].astype(BF)
            t2 = far(tg_d, gdn.at[b], t_send.at[1], t_recv.at[1], e, side)
            t2.start()
        if k:
            for d in at_step(k - 1):
                deliver(d)
    for d in at_step(n_up):
        deliver(d)
    ggu[b] = acc_u[:width, :].astype(BF)
    gdn[b] = acc_d[:, :width].astype(BF)

    landed(cb_r, c_recv)
    got = cb_r[...].astype(F32).reshape(ne, BLK, width)
    eo = got[:, :CAP].reshape(slots, width).astype(BF)
    dx = got[:, CAP:].reshape(slots, width).astype(BF)
    out[...] = (dot(whi[...], eo, 1, 0) + dot(wlo[...], eo, 1, 0)).astype(BF)
    gtok[...] = dot(place[...], dx, 1, 0).astype(BF)

    t1.wait_recv()
    t2.wait_recv()
    landed(disp.at[pl.ds(0, (ne - 1) * BLK)], d_send)
    landed(cb_s.at[pl.ds(0, (ne - 1) * BLK)], c_send)
    for move in (w1, w2, *moves, t1, t2):
        move.wait_send()
    for d in range(nz):
        landed(xo_s.at[d], o_send.at[d])
    for up, n in ((True, n_up), (False, n_dn)):
        for k in range(n):
            for c in range(3):
                if k < narrow:
                    src, at = (su_n if up else sd_n), k
                else:
                    src, at = (su_w if up else sd_w), k - narrow
                landed(src.at[c, at], (ru_send if up else rd_send).at[c, k])
                landed(act.at[c, pl.ds(0, share)], (gu_send if up else gd_send).at[c, k])


def body(tokens, out_grad, routes, scores, w_gate_up, w_down):
    ne, ndp = lax.axis_size("expert"), lax.axis_size("dp")
    nz = ndp // 2
    tok, width = tokens.shape
    hidden = w_down.shape[1]
    half = hidden // 2
    slots = ne * CAP
    share = slots // nz
    n_up, n_dn = nz // 2, nz // 2 - 1
    narrow = max(1, n_up - WIDE)
    ids = np.arange(slots)
    slot = jnp.asarray(np.stack([ids // CAP, ids % CAP]).astype(np.int32))
    lower = jnp.asarray(np.tril(np.ones((tok, tok), np.float32), -1)).astype(BF)
    wgu = w_gate_up[0].reshape(width, 2, 2, half).transpose(2, 0, 1, 3).reshape(2, width, 2 * half)
    wd = w_down[0].reshape(2, half, width)
    dma = pltpu.SemaphoreType.DMA
    ups = [pltpu.VMEM((3, narrow, share, half), BF)] * 2
    ups += [pltpu.VMEM((3, n_up - narrow, share, half), F32)] * 2
    dns = [pltpu.VMEM((3, narrow, share, half), BF)] * 2
    dns += [pltpu.VMEM((3, max(1, n_dn - narrow), share, half), F32)] * 2
    out, gtok, ggu, gdn = pl.pallas_call(
        functools.partial(kernel, ne, nz),
        out_shape=(
            jax.ShapeDtypeStruct((tok, width), BF),
            jax.ShapeDtypeStruct((tok, width), BF),
            jax.ShapeDtypeStruct((2, width, 2 * half), BF),
            jax.ShapeDtypeStruct((2, half, width), BF),
        ),
        in_specs=[pl.BlockSpec(memory_space=pltpu.VMEM)] * 8,
        out_specs=[pl.BlockSpec(memory_space=pltpu.VMEM)] * 4,
        scratch_shapes=[
            pltpu.VMEM((tok, slots), BF),
            pltpu.VMEM((tok, slots), BF),
            pltpu.VMEM((tok, slots), BF),
            pltpu.VMEM((ne * BLK, width), BF),
            pltpu.VMEM((2, ne * BLK, width), BF),
            pltpu.VMEM((slots, 2 * width), BF),
            pltpu.VMEM((slots, 2 * width), BF),
            pltpu.VMEM((2 * width, 2 * half), BF),
            pltpu.VMEM((half, width), BF),
            pltpu.VMEM((3, slots, half), F32),
            *ups,
            *dns,
            pltpu.VMEM((3, slots, half), BF),
            pltpu.VMEM((nz, 2 * share, width), BF),
            pltpu.VMEM((nz, 2 * share, width), BF),
            pltpu.VMEM((nz, 2 * share, width), F32),
            pltpu.VMEM((ne * BLK, width), BF),
            pltpu.VMEM((ne * BLK, width), BF),
            pltpu.VMEM((width, 2 * half), BF),
            pltpu.VMEM((half, width), BF),
            pltpu.VMEM((2 * width, 2 * half), F32),
            pltpu.VMEM((half, 2 * width), F32),
            dma, dma((GROUPS,)),
            dma((2,)), dma((2,)),
            dma((GROUPS,)), dma((GROUPS,)),
            dma((3, n_up)), dma((3, n_up)), dma((3, n_dn)), dma((3, n_dn)),
            dma((3, n_up)), dma((3, n_up)), dma((3, n_dn)), dma((3, n_dn)),
            dma((nz,)), dma((nz,)),
            dma, dma,
            dma((2,)), dma((2,)),
        ],
        compiler_params=pltpu.CompilerParams(
            collective_id=0, has_side_effects=True, vmem_limit_bytes=48 * 1024 * 1024
        ),
    )(routes, scores, tokens, out_grad, wgu, wd, slot, lower)
    grad_first = (
        ggu.reshape(2, width, 2, half).transpose(1, 2, 0, 3).reshape(1, width, 2, hidden)
    )
    return out, gtok, grad_first, gdn.reshape(1, hidden, width)


def solution(mesh):
    placed = (
        P("expert", "dp"),
        P("expert", "dp"),
        P("expert", None),
        P("expert", None),
        P("expert", "dp", None, None),
        P("expert", None, "dp"),
    )
    return jax.shard_map(
        body,
        mesh=mesh,
        in_specs=placed,
        out_specs=(
            P("expert", "dp"),
            P("expert", "dp"),
            P("expert", "dp", None, None),
            P("expert", None, "dp"),
        ),
        check_vma=False,
    )
```

```python
import functools

import jax
import jax.numpy as jnp
import numpy as np
from jax import lax
from jax.experimental import pallas as pl
from jax.experimental.pallas import tpu as pltpu
from jax.sharding import PartitionSpec as P

CAP = 24
BLK = 2 * CAP
GROUPS = 8
WIDE = 3
MESH = pl.DeviceIdType.MESH
BF = jnp.bfloat16
F32 = jnp.float32


def dot(a, b, ca, cb):
    return lax.dot_general(a, b, (((ca,), (cb,)), ((), ())), preferred_element_type=F32)


def landed(ref, sem):
    pltpu.make_async_copy(ref, ref, sem).wait()


def kernel(
    ne, nz, routes, scores, tokens, ograd, wgu, wd, slot, lower,
    out, gtok, ggu, gdn,
    place, whi, wlo, disp, rbuf, rows, grads, wgu2, wdp, part,
    su_n, ru_n, su_w, ru_w, sd_n, rd_n, sd_w, rd_w,
    act, xo_s, xo_r, own, cb_s, cb_r, tg_u, tg_d, acc_u, acc_d,
    d_send, d_recv, w_send, w_recv, f_send, f_recv,
    ru_send, ru_recv, rd_send, rd_recv, gu_send, gu_recv, gd_send, gd_recv,
    o_send, o_recv, c_send, c_recv, t_send, t_recv,
):
    e = lax.axis_index("expert")
    dp = lax.axis_index("dp")
    b = dp // nz
    z = lax.rem(dp, nz)
    side = (1 - b) * nz + z
    above = b * nz + lax.rem(z + 1, nz)
    below = b * nz + lax.rem(z + nz - 1, nz)
    slots = ne * CAP
    width = tokens.shape[1]
    half = wd.shape[1]
    share = slots // nz
    n_up, n_dn = nz // 2, nz // 2 - 1
    narrow = max(1, n_up - WIDE)
    per = ne // GROUPS
    mid = ne // 2

    def partner(i):
        to = lax.rem(e // mid + i // mid, 2) * mid + lax.rem(e + i, mid)
        return to, lax.rem(b + i // mid, 2) * nz + z

    def sender(i):
        to = lax.rem(e // mid + i // mid, 2) * mid + lax.rem(e + ne - i, mid)
        return to, lax.rem(b + i // mid, 2) * nz + z

    def far(src, dst, send, recv, to_e, to_dp):
        return pltpu.make_async_remote_copy(
            src_ref=src, dst_ref=dst, send_sem=send, recv_sem=recv,
            device_id=(to_e, to_dp), device_id_type=MESH,
        )

    barrier = pltpu.get_barrier_semaphore()

    def greet(i, c):
        pl.semaphore_signal(barrier, inc=1, device_id=partner(i), device_id_type=MESH)
        return c

    lax.fori_loop(1, ne, greet, 0)
    for to in (side, above, below):
        pl.semaphore_signal(barrier, inc=1, device_id=(e, to), device_id_type=MESH)

    pl.semaphore_wait(barrier, ne + 2)
    w1 = far(wgu.at[1 - b], wgu2.at[pl.ds(width, width)], w_send.at[0], w_recv.at[0], e, side)
    w2 = far(wd.at[1 - b], wdp, w_send.at[1], w_recv.at[1], e, side)
    w1.start()
    w2.start()

    combine = scores[...] / jnp.sum(scores[...], axis=1, keepdims=True)
    slot_e, slot_r = slot[0:1, :], slot[1:2, :]
    tok = tokens.shape[0]
    hit = jnp.zeros((tok, slots), F32)
    weight = jnp.zeros((tok, slots), F32)
    for j in range(routes.shape[1]):
        named = routes[:, j : j + 1] == slot_e
        hit = jnp.where(named, 1.0, hit)
        weight = jnp.where(named, combine[:, j : j + 1], weight)
    rank = dot(lower[...], hit.astype(BF), 1, 0)
    taken = jnp.where(rank == slot_r.astype(F32), hit, 0.0)
    weight = weight * taken
    place[...] = taken.astype(BF)
    high = weight.astype(BF)
    whi[...] = high
    wlo[...] = (weight - high.astype(F32)).astype(BF)

    send_rows = dot(place[...], tokens[...], 0, 0).reshape(ne, CAP, width)
    send_grad = dot(whi[...], ograd[...], 0, 0) + dot(wlo[...], ograd[...], 0, 0)
    both = jnp.concatenate([send_rows, send_grad.reshape(ne, CAP, width)], axis=1)
    disp[...] = both.reshape(ne * BLK, width).astype(BF)

    def block(i):
        return pl.ds(pl.multiple_of(i * BLK, BLK), BLK)

    def dispatch(i, c):
        to, col = partner(i)
        far(
            disp.at[block(to)], rbuf.at[i // mid, block(i)], d_send, d_recv.at[i // per], to, col
        ).start()
        return c

    lax.fori_loop(1, ne, dispatch, 0)
    pltpu.make_async_copy(disp.at[block(e)], rbuf.at[0, block(0)], d_recv.at[0]).start()

    wgu2[0:width, :] = wgu[b]
    moves = []
    for g in range(GROUPS):
        at = pl.ds(g * per * BLK, per * BLK)
        part_of = g * per // mid
        here, there = rbuf.at[part_of, at], rbuf.at[1 - part_of, at]
        landed(here, d_recv.at[g])
        move = far(here, there, f_send.at[g], f_recv.at[g], e, side)
        move.start()
        moves.append(move)

    def unpack(which, upper):
        at = pl.ds(upper * mid * BLK, mid * BLK)
        to = pl.ds(upper * mid * CAP, mid * CAP)
        got = rbuf[which, at, :].astype(F32).reshape(mid, BLK, width)
        cols = slice(which * width, (which + 1) * width)
        rows[to, cols] = got[:, :CAP].reshape(mid * CAP, width).astype(BF)
        grads[to, cols] = got[:, CAP:].reshape(mid * CAP, width).astype(BF)

    unpack(0, 0)
    unpack(1, 1)
    w1.wait_recv()
    w2.wait_recv()
    for move in moves[: GROUPS // 2]:
        move.wait_recv()
    unpack(1, 0)
    for move in moves[GROUPS // 2 :]:
        move.wait_recv()
    unpack(0, 1)

    step = slots // 4
    wd2 = jnp.concatenate([wd[b], wdp[...]], axis=1)

    def partial(i, c):
        at = pl.ds(pl.multiple_of(i * step, step), step)
        value = dot(rows[at, :], wgu2[...], 1, 0)
        part[0, at, :] = value[:, :half]
        part[1, at, :] = value[:, half:]
        part[2, at, :] = dot(grads[at, :], wd2, 1, 1)
        return c

    lax.fori_loop(0, 4, partial, 0)

    def of(d):
        return pl.ds(pl.multiple_of(d * share, share), share)

    def sums(up, k, c):
        n = n_up if up else n_dn
        if k < 0 or k >= n:
            return
        d = lax.rem(z + n_up - k, nz) if up else lax.rem(z + nz - n_dn + k, nz)
        send, recv = (ru_send, ru_recv) if up else (rd_send, rd_recv)
        value = part[c, of(d), :]
        if k:
            value = value + arrived(up, k - 1, c)
        if k < narrow:
            src, dst, at = (su_n, ru_n, k) if up else (sd_n, rd_n, k)
        else:
            src, dst, at = (su_w, ru_w, k - narrow) if up else (sd_w, rd_w, k - narrow)
        src[c, at] = value.astype(src.dtype)
        far(
            src.at[c, at], dst.at[c, at], send.at[c, k], recv.at[c, k],
            e, above if up else below,
        ).start()

    def arrived(up, k, c):
        if k < narrow:
            ref, at = (ru_n if up else rd_n), k
        else:
            ref, at = (ru_w if up else rd_w), k - narrow
        landed(ref.at[c, at], (ru_recv if up else rd_recv).at[c, k])
        return ref[c, at].astype(F32)

    def summed(c):
        return part[c, of(z), :] + arrived(False, n_dn - 1, c) + arrived(True, n_up - 1, c)

    def gathers(up, k, c):
        n = n_up if up else n_dn
        if k < 0 or k > n:
            return
        d = lax.rem(z + nz - k, nz) if up else lax.rem(z + k, nz)
        send, recv = (gu_send, gu_recv) if up else (gd_send, gd_recv)
        at = act.at[c, of(d)]
        if k:
            landed(at, recv.at[c, k - 1])
        if k < n:
            far(at, at, send.at[c, k], recv.at[c, k], e, above if up else below).start()

    def finish(d, first):
        hid = act[0, of(d), :]
        both = jnp.concatenate([act[1, of(d), :], act[2, of(d), :]], axis=1)
        eo = dot(hid, jnp.concatenate([wd[b], wdp[...]], axis=1), 1, 0)
        dx = dot(both, wgu2[...], 1, 1)
        mine = jnp.concatenate([eo[:, :width], dx[:, :width]], axis=0)
        other = jnp.concatenate([eo[:, width:], dx[:, width:]], axis=0)

        @pl.when(d < nz // 2)
        def _():
            own[d] = mine
            xo_s[d] = other.astype(BF)

        @pl.when(d >= nz // 2)
        def _():
            own[d] = other
            xo_s[d] = mine.astype(BF)

        far(xo_s.at[d], xo_r.at[d], o_send.at[d], o_recv.at[d], e, side).start()
        to_u = dot(rows[of(d), :], both, 0, 0)
        to_d = dot(hid, grads[of(d), :], 0, 0)
        acc_u[...] = to_u if first else acc_u[...] + to_u
        acc_d[...] = to_d if first else acc_d[...] + to_d

    n_blk = share // CAP

    def deliver(d):
        landed(xo_r.at[d], o_recv.at[d])
        got = own[d] + xo_r[d].astype(F32)
        eo = got[:share].reshape(n_blk, CAP, width)
        dx = got[share:].reshape(n_blk, CAP, width)
        whole = jnp.concatenate([eo, dx], axis=1).reshape(n_blk * BLK, width)
        cb_s[pl.ds(pl.multiple_of(d * n_blk * BLK, n_blk * BLK), n_blk * BLK), :] = whole.astype(BF)
        for i in range(n_blk):
            p = d * n_blk + i
            to, col = sender(p)

            @pl.when(p != 0)
            def _():
                far(cb_s.at[block(p)], cb_r.at[block(e)], c_send, c_recv, to, col).start()

            @pl.when(p == 0)
            def _():
                pltpu.make_async_copy(cb_s.at[block(p)], cb_r.at[block(e)], c_recv).start()

    def at_step(k):
        if k == 0:
            return [z]
        if k > n_dn:
            return [lax.rem(z + nz - k, nz)]
        return [lax.rem(z + nz - k, nz), lax.rem(z + k, nz)]

    for k in range(n_up):
        for c in range(3):
            sums(True, k, c)
            sums(False, k, c)
    gate, upper, grad_hidden = summed(0), summed(1), summed(2)
    sig = jax.nn.sigmoid(gate)
    act[0, of(z), :] = (gate * sig * upper).astype(BF)
    act[1, of(z), :] = (grad_hidden * upper * sig * (1.0 + gate * (1.0 - sig))).astype(BF)
    act[2, of(z), :] = (grad_hidden * (gate * sig)).astype(BF)
    for k in range(n_up + 1):
        for c in range(3):
            gathers(True, k, c)
            gathers(False, k, c)
        for d in at_step(k):
            finish(d, k == 0)
        if k == n_up:
            tg_u[...] = acc_u[width:, :].astype(BF)
            t1 = far(tg_u, ggu.at[b], t_send.at[0], t_recv.at[0], e, side)
            t1.start()
            tg_d[...] = acc_d[:, width:].astype(BF)
            t2 = far(tg_d, gdn.at[b], t_send.at[1], t_recv.at[1], e, side)
            t2.start()
        if k:
            for d in at_step(k - 1):
                deliver(d)
    for d in at_step(n_up):
        deliver(d)
    ggu[b] = acc_u[:width, :].astype(BF)
    gdn[b] = acc_d[:, :width].astype(BF)

    landed(cb_r, c_recv)
    got = cb_r[...].astype(F32).reshape(ne, BLK, width)
    eo = got[:, :CAP].reshape(slots, width).astype(BF)
    dx = got[:, CAP:].reshape(slots, width).astype(BF)
    out[...] = (dot(whi[...], eo, 1, 0) + dot(wlo[...], eo, 1, 0)).astype(BF)
    gtok[...] = dot(place[...], dx, 1, 0).astype(BF)

    t1.wait_recv()
    t2.wait_recv()
    landed(disp.at[pl.ds(0, (ne - 1) * BLK)], d_send)
    landed(cb_s.at[pl.ds(0, (ne - 1) * BLK)], c_send)
    for move in (w1, w2, *moves, t1, t2):
        move.wait_send()
    for d in range(nz):
        landed(xo_s.at[d], o_send.at[d])
    for up, n in ((True, n_up), (False, n_dn)):
        for k in range(n):
            for c in range(3):
                if k < narrow:
                    src, at = (su_n if up else sd_n), k
                else:
                    src, at = (su_w if up else sd_w), k - narrow
                landed(src.at[c, at], (ru_send if up else rd_send).at[c, k])
                landed(act.at[c, pl.ds(0, share)], (gu_send if up else gd_send).at[c, k])


def body(tokens, out_grad, routes, scores, w_gate_up, w_down):
    ne, ndp = lax.axis_size("expert"), lax.axis_size("dp")
    nz = ndp // 2
    tok, width = tokens.shape
    hidden = w_down.shape[1]
    half = hidden // 2
    slots = ne * CAP
    share = slots // nz
    n_up, n_dn = nz // 2, nz // 2 - 1
    narrow = max(1, n_up - WIDE)
    ids = np.arange(slots)
    slot = jnp.asarray(np.stack([ids // CAP, ids % CAP]).astype(np.int32))
    lower = jnp.asarray(np.tril(np.ones((tok, tok), np.float32), -1)).astype(BF)
    wgu = w_gate_up[0].reshape(width, 2, 2, half).transpose(2, 0, 1, 3).reshape(2, width, 2 * half)
    wd = w_down[0].reshape(2, half, width)
    dma = pltpu.SemaphoreType.DMA
    ups = [pltpu.VMEM((3, narrow, share, half), BF)] * 2
    ups += [pltpu.VMEM((3, n_up - narrow, share, half), F32)] * 2
    dns = [pltpu.VMEM((3, narrow, share, half), BF)] * 2
    dns += [pltpu.VMEM((3, max(1, n_dn - narrow), share, half), F32)] * 2
    out, gtok, ggu, gdn = pl.pallas_call(
        functools.partial(kernel, ne, nz),
        out_shape=(
            jax.ShapeDtypeStruct((tok, width), BF),
            jax.ShapeDtypeStruct((tok, width), BF),
            jax.ShapeDtypeStruct((2, width, 2 * half), BF),
            jax.ShapeDtypeStruct((2, half, width), BF),
        ),
        in_specs=[pl.BlockSpec(memory_space=pltpu.VMEM)] * 8,
        out_specs=[pl.BlockSpec(memory_space=pltpu.VMEM)] * 4,
        scratch_shapes=[
            pltpu.VMEM((tok, slots), BF),
            pltpu.VMEM((tok, slots), BF),
            pltpu.VMEM((tok, slots), BF),
            pltpu.VMEM((ne * BLK, width), BF),
            pltpu.VMEM((2, ne * BLK, width), BF),
            pltpu.VMEM((slots, 2 * width), BF),
            pltpu.VMEM((slots, 2 * width), BF),
            pltpu.VMEM((2 * width, 2 * half), BF),
            pltpu.VMEM((half, width), BF),
            pltpu.VMEM((3, slots, half), F32),
            *ups,
            *dns,
            pltpu.VMEM((3, slots, half), BF),
            pltpu.VMEM((nz, 2 * share, width), BF),
            pltpu.VMEM((nz, 2 * share, width), BF),
            pltpu.VMEM((nz, 2 * share, width), F32),
            pltpu.VMEM((ne * BLK, width), BF),
            pltpu.VMEM((ne * BLK, width), BF),
            pltpu.VMEM((width, 2 * half), BF),
            pltpu.VMEM((half, width), BF),
            pltpu.VMEM((2 * width, 2 * half), F32),
            pltpu.VMEM((half, 2 * width), F32),
            dma, dma((GROUPS,)),
            dma((2,)), dma((2,)),
            dma((GROUPS,)), dma((GROUPS,)),
            dma((3, n_up)), dma((3, n_up)), dma((3, n_dn)), dma((3, n_dn)),
            dma((3, n_up)), dma((3, n_up)), dma((3, n_dn)), dma((3, n_dn)),
            dma((nz,)), dma((nz,)),
            dma, dma,
            dma((2,)), dma((2,)),
        ],
        compiler_params=pltpu.CompilerParams(
            collective_id=0, has_side_effects=True, vmem_limit_bytes=48 * 1024 * 1024
        ),
    )(routes, scores, tokens, out_grad, wgu, wd, slot, lower)
    grad_first = (
        ggu.reshape(2, width, 2, half).transpose(1, 2, 0, 3).reshape(1, width, 2, hidden)
    )
    return out, gtok, grad_first, gdn.reshape(1, hidden, width)


def solution(mesh):
    placed = (
        P("expert", "dp"),
        P("expert", "dp"),
        P("expert", None),
        P("expert", None),
        P("expert", "dp", None, None),
        P("expert", None, "dp"),
    )
    return jax.shard_map(
        body,
        mesh=mesh,
        in_specs=placed,
        out_specs=(
            P("expert", "dp"),
            P("expert", "dp"),
            P("expert", "dp", None, None),
            P("expert", None, "dp"),
        ),
        check_vma=False,
    )
```
